512 devices in a mesh: dom: 64 (over y, z), rep: 8 (over x, core).
Axes of the slice: x: 4, y: 4, z: 16, core: 2. Of those that a mesh axis runs over, the one named last changes fastest.
Arguments:
- feats: bfloat16 [256, 32768], P('rep', 'dom'), may hold values from -6 to 6
- weight: bfloat16 [256, 256], P(None, 'rep'), may hold values from -0.375 to 0.375
- tile_values: bfloat16 [8192, 128, 128], P('dom'), may hold values from -0.09375 to 0.09375
- tile_dest: int32 [8192, 1], P('dom'), may hold values from 0 to 63; in each aligned block of 128 rows (0 to 127, 128 to 255, ...) at most 4 rows name the same one
- tile_block: int32 [8192], P('dom'), may hold values from 0 to 3
- tile_source: int32 [8192], P('dom'), may hold values from 0 to 3
- cotangent: bfloat16 [256, 32768], P('rep', 'dom'), may hold values from -6 to 6
Outputs:
- hidden: bfloat16 [256, 32768], P('rep', 'dom')
- weight_grad: float32 [256, 256], P(None, 'rep')
- input_grad: bfloat16 [256, 32768], P('rep', 'dom')
The draws below stay inside these ranges and needn't reach their ends.
Inputs may be any that keep to these rules, and one draw needn't show every extreme that they name: `tile_dest`: among the 128 tiles of one index of dom at most 4 name the same owner, and some owner is named 4 times.
All inputs are finite; a program needn't handle non-finite values.
Results may differ from the reference program's by a relative error of at most 0.0065.
Values may be sent and summed in bfloat16 or wider, within the bound.
No kernel may reach another device: no remote copies, remote signals or barrier semaphores. Data moves between devices by JAX's collectives and lax.ppermute only.
A program may use at most 64 MiB of HBM per device.

```python
import math
import jax
import jax.numpy as jnp
import numpy as np
from jax import lax

F = 256
BLK = 128
NB = 4
TILE_DEV = 128
CAP = 4
NODES = 32768
TILES = 8192
N_DOM = 64


def set_ends(drawn, stream_key, low, top_value):
    place = [jax.random.randint(jax.random.fold_in(stream_key, axis), (), 0, length) for axis, length in enumerate(drawn.shape)]
    main_axis = drawn.shape.index(max(drawn.shape))
    beside = place[:main_axis] + [(place[main_axis] + 1) % drawn.shape[main_axis]] + place[main_axis + 1:]
    return drawn.at[tuple(place)].set(low).at[tuple(beside)].set(top_value)


def block_scale(stream_key, extent, split, smallest, largest):
    def one(dim, parts):
        heights = jax.random.uniform(jax.random.fold_in(jax.random.fold_in(stream_key, 6), dim), (parts,), jnp.float32, smallest / len(split), largest / len(split))
        return jnp.repeat(jnp.exp(heights), extent[dim] // parts).reshape((-1,) + (1,) * (len(extent) - dim - 1))

    level = one(*split[0])
    for cut in split[1:]:
        level = level * one(*cut)
    return level


def routed_block(rng, own, number, rows, number_of, top, reach, skew):
    sequence = jax.random.permutation(rng, number_of)
    crowded, common = load_shares(number_of, rows * top, reach, skew, True), load_shares(number_of, rows * top, reach, skew, False)
    places = jnp.arange(number_of)

    def named(sizes, rotation):
        used = int((sizes > 0).sum())
        fixed = max(1, used // 4)
        shifted = fixed + (places - fixed + rotation * (used - fixed)) % max(1, number_of - fixed)
        return jnp.zeros((number_of,), jnp.int32).at[sequence[jnp.where(places < fixed, places, shifted)]].set(jnp.asarray(sizes, jnp.int32))

    sizes = jnp.where(number % 4 == 0, named(crowded, number // 4), named(common, number - number // 4 - 1))
    mixed = jax.random.permutation(jax.random.fold_in(own, 3), number_of)
    donor, sink = mixed[0:number_of // 2 * 2:2], mixed[1:number_of // 2 * 2:2]
    margin = jnp.minimum(sizes[donor] - 1, reach - sizes[sink]) // 2
    margin = jnp.where((donor == sequence[0]) | (sink == sequence[0]) | (sizes[sink] == 0), 0, jnp.maximum(margin, 0))
    shifted = jax.random.randint(jax.random.fold_in(own, 4), (number_of // 2,), 0, 1 << 20) % (margin + 1)
    sizes = sizes.at[donor].add(-shifted).at[sink].add(shifted)
    items = jnp.searchsorted(jnp.cumsum(sizes), jnp.arange(rows * top), side="right").astype(jnp.int32)
    table = items.reshape(top, rows).T
    table = table[jax.random.permutation(jax.random.fold_in(own, 1), rows)]
    rotation = jax.random.randint(jax.random.fold_in(own, 2), (rows, 1), 0, top)
    return jnp.take_along_axis(table, (jnp.arange(top)[None, :] + rotation) % top, axis=1)


def load_shares(count, total, reach, slope, full):
    weights = [(1 << 20) // math.isqrt(rank ** slope) + 1 for rank in range(1, count + 1)]
    largest = reach if full else min(reach, max(-(-total // count), total * weights[0] // sum(weights)))
    least = 1 if total - largest >= count - 1 else 0
    holding, rest = [largest] + [least] * (count - 1), total - largest - least * (count - 1)
    while rest > 0:
        candidates = [i for i in range(1, count) if holding[i] < largest] or [i for i in range(1, count) if holding[i] < reach]
        whole, budget = sum([weights[i] for i in candidates]), rest
        for i in candidates:
            extra = min(reach - holding[i], max(1, budget * weights[i] // whole), rest)
            holding[i] = holding[i] + extra
            rest = rest - extra
    return np.array(holding)


def bell_draw(stream_key, dims, width, reach, shards=(), kind=jnp.bfloat16):
    array = width * jax.random.normal(stream_key, dims, jnp.float32)
    if shards:
        array = array * block_scale(stream_key, dims, shards, -0.22, 0.18)
    return jnp.clip(array, -reach, reach).astype(kind)


def setup_inputs(seed: int = 0) -> dict:
    keys = jax.random.split(jax.random.key(seed), 8)
    feats = bell_draw(keys[0], (F, NODES), 1.0, 6.0, ((0, 8), (1, 64)))
    weight = bell_draw(keys[1], (F, F), F ** -0.5, 0.375, ((1, 8),))
    tile_values = bell_draw(keys[2], (TILES, BLK, BLK), (BLK * TILE_DEV // NB) ** -0.5, 0.09375, ((0, 64),))
    tile_dest_keys = jax.random.split(jax.random.fold_in(keys[3], 1), TILES // TILE_DEV)
    tile_dest_turns = jax.random.permutation(jax.random.fold_in(keys[3], 3), TILES // TILE_DEV)
    tile_dest = jax.vmap(lambda own, number: routed_block(jax.random.fold_in(keys[3], 2), own, number, TILE_DEV, N_DOM, 1, CAP, 1))(tile_dest_keys, tile_dest_turns).reshape((TILES, 1))
    tile_block = set_ends(jax.random.randint(keys[4], (TILES,), 0, NB), jax.random.fold_in(keys[4], 1), 0, NB - 1).astype(jnp.int32)
    tile_source = set_ends(jax.random.randint(keys[5], (TILES,), 0, NB), jax.random.fold_in(keys[5], 1), 0, NB - 1).astype(jnp.int32)
    cotangent = bell_draw(keys[6], (F, NODES), 1.0, 6.0, ((0, 8), (1, 64)))
    return {"feats": feats, "weight": weight, "tile_values": tile_values, "tile_dest": tile_dest, "tile_block": tile_block, "tile_source": tile_source, "cotangent": cotangent}


def reference(feats, weight, tile_values, tile_dest, tile_block, tile_source, cotangent):
    nblk_all = NODES // BLK
    projected = jnp.dot(weight.T, feats, preferred_element_type=jnp.float32).astype(jnp.bfloat16)
    proj_blocks = projected.reshape(F, nblk_all, BLK).transpose(1, 0, 2)
    owner = jnp.arange(TILES, dtype=jnp.int32) // TILE_DEV
    dest = (tile_dest[:, 0] * NB + tile_block).astype(jnp.int32)
    source = (owner * NB + tile_source).astype(jnp.int32)
    tiles = tile_values.reshape(N_DOM, TILE_DEV, BLK, BLK)
    dests = dest.reshape(N_DOM, TILE_DEV)
    sources = source.reshape(N_DOM, TILE_DEV)

    def forward_step(total, item):
        values, to_block, from_block = item
        prods = jnp.einsum('tfc,trc->tfr', proj_blocks[from_block].astype(jnp.float32),
                           values.astype(jnp.float32), precision=lax.Precision.HIGHEST)
        return total.at[to_block].add(prods), None

    mixed_blocks, _ = lax.scan(forward_step, jnp.zeros((nblk_all, F, BLK), jnp.float32), (tiles, dests, sources))
    mixed = mixed_blocks.transpose(1, 0, 2).reshape(F, NODES)
    sig = jax.nn.sigmoid(mixed)
    hidden = (mixed * sig).astype(jnp.bfloat16)
    delta = (cotangent.astype(jnp.float32) * sig * (1.0 + mixed * (1.0 - sig))).astype(jnp.bfloat16)
    delta_blocks = delta.reshape(F, nblk_all, BLK).transpose(1, 0, 2)

    def backward_step(total, item):
        values, to_block, from_block = item
        prods = jnp.einsum('tfr,trc->tfc', delta_blocks[to_block].astype(jnp.float32),
                           values.astype(jnp.float32), precision=lax.Precision.HIGHEST)
        return total.at[from_block].add(prods), None

    back_blocks, _ = lax.scan(backward_step, jnp.zeros((nblk_all, F, BLK), jnp.float32), (tiles, dests, sources))
    back = back_blocks.transpose(1, 0, 2).reshape(F, NODES).astype(jnp.bfloat16)
    weight_grad = jnp.dot(feats, back.T, preferred_element_type=jnp.float32) * (float(NODES) ** -0.5)
    input_grad = jnp.dot(weight, back, preferred_element_type=jnp.float32).astype(jnp.bfloat16)
    return hidden, weight_grad, input_grad
```

```python
import functools

import jax
import jax.numpy as jnp
from jax import lax
from jax.experimental import pallas as pl
from jax.experimental.pallas import tpu as pltpu
from jax.sharding import Mesh, PartitionSpec as P

BF = jnp.bfloat16
F32 = jnp.float32
NY, NZ, NX, NC = 4, 16, 4, 2
BLK = 128
GROUP = 16


def scatter_products(slot_ref, src_ref, feats_ref, tiles_ref, out_ref, acc_ref):
    step = pl.program_id(0)

    @pl.when(step == 0)
    def _():
        acc_ref[...] = jnp.zeros_like(acc_ref)

    for k in range(GROUP):
        t = step * GROUP + k
        col = pl.multiple_of(src_ref[t] * BLK, BLK)
        prod = lax.dot_general(
            feats_ref[:, pl.ds(col, BLK)],
            tiles_ref[k],
            (((1,), (1,)), ((), ())),
            preferred_element_type=F32,
        )
        acc_ref[slot_ref[t]] += prod

    @pl.when(step == pl.num_programs(0) - 1)
    def _():
        out_ref[...] = acc_ref[...].astype(BF)


def gather_products(slot_ref, src_ref, every_ref, tiles_ref, out_ref, acc_ref):
    step = pl.program_id(0)

    @pl.when(step == 0)
    def _():
        acc_ref[...] = jnp.zeros_like(acc_ref)

    for k in range(GROUP):
        t = step * GROUP + k
        prod = jnp.dot(every_ref[slot_ref[t]], tiles_ref[k], preferred_element_type=F32)
        acc_ref[src_ref[t]] += prod

    @pl.when(step == pl.num_programs(0) - 1)
    def _():
        for b in range(acc_ref.shape[0]):
            out_ref[:, b * BLK : (b + 1) * BLK] = acc_ref[b].astype(BF)


def middle(rep_ref, g_ref, wt_ref, wrows_ref, cot_ref, hid_ref, grad_ref, wg_ref, all_ref, del_ref, mix_ref):
    rep = rep_ref[0]
    reps, blocks, panel, _ = g_ref.shape
    for r in range(reps):
        for b in range(blocks):
            all_ref[r * panel : (r + 1) * panel, b * BLK : (b + 1) * BLK] = g_ref[r, b]
    mixed = jnp.dot(wt_ref[...], all_ref[...], preferred_element_type=F32)
    mix_ref[...] = mixed
    sig = jax.nn.sigmoid(mixed)
    delta = cot_ref[...].astype(F32) * sig * (1.0 + mixed * (1.0 - sig))
    del_ref[...] = delta.astype(BF)
    sent = jnp.dot(wrows_ref[...], del_ref[...], preferred_element_type=F32)
    for b in range(blocks):
        grad_ref[b] = sent[:, b * BLK : (b + 1) * BLK].astype(BF)
    own = pl.ds(pl.multiple_of(rep * panel, panel), panel)
    mine = mix_ref[own, :]
    hid_ref[...] = (mine * jax.nn.sigmoid(mine)).astype(BF)
    wg_ref[...] = lax.dot_general(
        del_ref[own, :], all_ref[...], (((1,), (1,)), ((), ())), preferred_element_type=F32
    )


def per_device(feats, weight, tile_values, tile_dest, tile_block, tile_source, cotangent):
    panel, rows = feats.shape
    tiles = tile_values.shape[0]
    nblk = rows // BLK
    ntot = NY * NZ * nblk
    reps = NX * NC
    rep = lax.axis_index(("x", "core"))
    slot = tile_dest[:, 0] * nblk + tile_block

    weight_t = weight.T
    both = lax.all_gather(
        jnp.concatenate([cotangent, weight_t], axis=1), ("x", "core"), axis=0, tiled=True
    )
    cot_all = both[:, :rows]
    wt_all = both[:, rows:]
    w_rows = lax.dynamic_slice_in_dim(wt_all, rep * panel, panel, axis=1).T

    parts = pl.pallas_call(
        scatter_products,
        grid_spec=pltpu.PrefetchScalarGridSpec(
            num_scalar_prefetch=2,
            grid=(tiles // GROUP,),
            in_specs=[
                pl.BlockSpec((panel, rows), lambda i, *_: (0, 0)),
                pl.BlockSpec((GROUP, BLK, BLK), lambda i, *_: (i, 0, 0)),
            ],
            out_specs=pl.BlockSpec((ntot, panel, BLK), lambda i, *_: (0, 0, 0)),
            scratch_shapes=[pltpu.VMEM((ntot, panel, BLK), F32)],
        ),
        out_shape=jax.ShapeDtypeStruct((ntot, panel, BLK), BF),
        compiler_params=pltpu.CompilerParams(vmem_limit_bytes=40 * 1024 * 1024),
        cost_estimate=pl.CostEstimate(
            flops=2 * tiles * panel * BLK * BLK,
            bytes_accessed=tiles * BLK * BLK * 2 + ntot * panel * BLK * 2,
            transcendentals=0,
        ),
        name="scatter_products",
    )(slot, tile_source, feats, tile_values)

    got = lax.all_to_all(parts.reshape(NY, NZ * nblk, panel, BLK), "y", 0, 0)
    half = jnp.sum(got.astype(F32), axis=0).astype(BF)
    got = lax.all_to_all(half.reshape(NZ, nblk, panel, BLK), "z", 0, 0)
    gathered = jnp.sum(got.astype(F32), axis=0).astype(BF)
    g_all = lax.all_gather(gathered, ("x", "core"), axis=0)

    hidden, sent, wgrad = pl.pallas_call(
        middle,
        grid_spec=pltpu.PrefetchScalarGridSpec(
            num_scalar_prefetch=1,
            grid=(1,),
            in_specs=[
                pl.BlockSpec((reps, nblk, panel, BLK), lambda i, *_: (0, 0, 0, 0)),
                pl.BlockSpec((reps * panel, reps * panel), lambda i, *_: (0, 0)),
                pl.BlockSpec((panel, reps * panel), lambda i, *_: (0, 0)),
                pl.BlockSpec((reps * panel, rows), lambda i, *_: (0, 0)),
            ],
            out_specs=[
                pl.BlockSpec((panel, rows), lambda i, *_: (0, 0)),
                pl.BlockSpec((nblk, panel, BLK), lambda i, *_: (0, 0, 0)),
                pl.BlockSpec((panel, reps * panel), lambda i, *_: (0, 0)),
            ],
            scratch_shapes=[
                pltpu.VMEM((reps * panel, rows), BF),
                pltpu.VMEM((reps * panel, rows), BF),
                pltpu.VMEM((reps * panel, rows), F32),
            ],
        ),
        out_shape=[
            jax.ShapeDtypeStruct((panel, rows), BF),
            jax.ShapeDtypeStruct((nblk, panel, BLK), BF),
            jax.ShapeDtypeStruct((panel, reps * panel), F32),
        ],
        compiler_params=pltpu.CompilerParams(vmem_limit_bytes=40 * 1024 * 1024),
        cost_estimate=pl.CostEstimate(
            flops=2 * (reps * panel) ** 2 * rows, bytes_accessed=1 << 20, transcendentals=reps * panel * rows
        ),
        name="middle",
    )(rep.reshape(1).astype(jnp.int32), g_all, wt_all, w_rows, cot_all)

    col = lax.all_to_all(jnp.broadcast_to(sent[None], (NZ, *sent.shape)), "z", 0, 0)
    every = lax.all_to_all(jnp.broadcast_to(col[None], (NY, *col.shape)), "y", 0, 0)
    every = every.reshape(ntot, panel, BLK)

    wsum = jnp.sum(lax.all_gather(wgrad, "y", axis=0), axis=0).astype(BF)
    wsum = jnp.sum(
        lax.all_to_all(jnp.broadcast_to(wsum[None], (NZ, *wsum.shape)), "z", 0, 0).astype(F32), axis=0
    )
    weight_grad = (wsum * float(rows * NY * NZ) ** (-0.5)).T

    input_grad = pl.pallas_call(
        gather_products,
        grid_spec=pltpu.PrefetchScalarGridSpec(
            num_scalar_prefetch=2,
            grid=(tiles // GROUP,),
            in_specs=[
                pl.BlockSpec((ntot, panel, BLK), lambda i, *_: (0, 0, 0)),
                pl.BlockSpec((GROUP, BLK, BLK), lambda i, *_: (i, 0, 0)),
            ],
            out_specs=pl.BlockSpec((panel, rows), lambda i, *_: (0, 0)),
            scratch_shapes=[pltpu.VMEM((nblk, panel, BLK), F32)],
        ),
        out_shape=jax.ShapeDtypeStruct((panel, rows), BF),
        compiler_params=pltpu.CompilerParams(vmem_limit_bytes=40 * 1024 * 1024),
        cost_estimate=pl.CostEstimate(
            flops=2 * tiles * panel * BLK * BLK,
            bytes_accessed=tiles * BLK * BLK * 2 + ntot * panel * BLK * 2,
            transcendentals=0,
        ),
        name="gather_products",
    )(slot, tile_source, every, tile_values)
    return hidden, weight_grad, input_grad


def solution(mesh):
    split = Mesh(mesh.devices.reshape(NY, NZ, NX, NC), ("y", "z", "x", "core"))
    dom, rep = ("y", "z"), ("x", "core")
    placed = (P(rep, dom), P(None, rep), P(dom, None, None), P(dom, None), P(dom), P(dom), P(rep, dom))
    return jax.shard_map(
        per_device,
        mesh=split,
        in_specs=placed,
        out_specs=(P(rep, dom), P(None, rep), P(rep, dom)),
        check_vma=False,
    )
```

```python
import jax
import jax.numpy as jnp
from jax import lax
from jax.experimental import pallas as pl
from jax.experimental.pallas import tpu as pltpu
from jax.sharding import Mesh, PartitionSpec as P

BF = jnp.bfloat16
F32 = jnp.float32
NY, NZ, NX, NC = 4, 16, 4, 2
BLK = 128
CHUNKS = 8
NZ8, NP = NZ // 2, 2

SMEM = pl.BlockSpec(memory_space=pltpu.SMEM)
VMEM = pl.BlockSpec(memory_space=pltpu.VMEM)
HBM = pl.BlockSpec(memory_space=pltpu.HBM)


def in_hbm(x):
    return pltpu.with_memory_space_constraint(x, pltpu.HBM)


def slot(dest, block, nblk):
    y, z = dest // NZ, dest % NZ
    return (((y * NP) + z % NP) * NZ8 + z // NP) * nblk + block


def call(kernel, name, out_shape, in_specs, scratch=(), mib=24, flops=0, nbytes=0, outs=None):
    outs = outs or jax.tree.map(lambda _: VMEM, out_shape)
    return pl.pallas_call(
        kernel,
        name=name,
        out_shape=out_shape,
        in_specs=in_specs,
        out_specs=outs,
        scratch_shapes=list(scratch),
        compiler_params=pltpu.CompilerParams(vmem_limit_bytes=mib << 20),
        cost_estimate=pl.CostEstimate(flops=flops, bytes_accessed=nbytes, transcendentals=0),
    )


def tile_copies(tiles_ref, buf_ref, sems):
    n = tiles_ref.shape[0] // CHUNKS
    return [
        pltpu.make_async_copy(tiles_ref.at[pl.ds(c * n, n)], buf_ref.at[pl.ds(c * n, n)], sems.at[c])
        for c in range(CHUNKS)
    ]


def scatter_products(dest_ref, block_ref, src_ref, feats_ref, tiles_ref, out_ref, acc_ref, half_ref, buf_ref, sems, out_sems):
    copies = tile_copies(tiles_ref, buf_ref, sems)
    for c in copies:
        c.start()
    acc_ref[...] = jnp.zeros_like(acc_ref)
    n = tiles_ref.shape[0] // CHUNKS
    nblk = feats_ref.shape[1] // BLK
    for c in range(CHUNKS):
        copies[c].wait()
        for t in range(c * n, (c + 1) * n):
            col = pl.multiple_of(src_ref[t] * BLK, BLK)
            prod = lax.dot_general(
                feats_ref[:, pl.ds(col, BLK)],
                buf_ref[t],
                (((1,), (1,)), ((), ())),
                preferred_element_type=F32,
            )
            acc_ref[slot(dest_ref[t], block_ref[t], nblk)] += prod
    m = out_ref.shape[0] // CHUNKS
    writes = []
    for c in range(CHUNKS):
        part = pl.ds(c * m, m)
        half_ref[part] = acc_ref[part].astype(BF)
        writes.append(pltpu.make_async_copy(half_ref.at[part], out_ref.at[part], out_sems.at[c]))
        writes[c].start()
    for c in range(CHUNKS):
        writes[c].wait()


def gather_products(dest_ref, block_ref, src_ref, every_ref, tiles_ref, out_ref, acc_ref, buf_ref, sems):
    copies = tile_copies(tiles_ref, buf_ref, sems)
    for c in copies:
        c.start()
    acc_ref[...] = jnp.zeros_like(acc_ref)
    n = tiles_ref.shape[0] // CHUNKS
    nblk = acc_ref.shape[0]
    for c in range(CHUNKS):
        copies[c].wait()
        for t in range(c * n, (c + 1) * n):
            prod = jnp.dot(
                every_ref[slot(dest_ref[t], block_ref[t], nblk)], buf_ref[t], preferred_element_type=F32
            )
            acc_ref[src_ref[t]] += prod
    for b in range(nblk):
        out_ref[:, b * BLK : (b + 1) * BLK] = acc_ref[b].astype(BF)


def sum_first(got_ref, out_ref):
    total = got_ref[0].astype(F32)
    for k in range(1, got_ref.shape[0]):
        total += got_ref[k].astype(F32)
    out_ref[...] = total.astype(BF)


def finish_sum(got_ref, out_ref):
    for b in range(got_ref.shape[1]):
        total = got_ref[0, b].astype(F32)
        for k in range(1, got_ref.shape[0]):
            total += got_ref[k, b].astype(F32)
        total = total.astype(BF)
        for r in range(out_ref.shape[0]):
            out_ref[r, b] = total


def middle(rep_ref, got_ref, both_ref, hid_ref, msg_ref, wg_ref, all_ref, del_ref, mix_ref):
    reps, nblk, panel, _ = got_ref.shape
    rows = nblk * BLK
    for r in range(reps):
        for b in range(nblk):
            all_ref[r * panel : (r + 1) * panel, b * BLK : (b + 1) * BLK] = got_ref[r, b]
    own = pl.ds(pl.multiple_of(rep_ref[0] * panel, panel), panel)
    weight = both_ref[:, rows:]
    mixed = jnp.dot(weight, all_ref[...], preferred_element_type=F32)
    mix_ref[...] = mixed
    sig = jax.nn.sigmoid(mixed)
    delta = both_ref[:, :rows].astype(F32) * sig * (1.0 + mixed * (1.0 - sig))
    del_ref[...] = delta.astype(BF)
    mine = mix_ref[own, :]
    hid_ref[...] = (mine * jax.nn.sigmoid(mine)).astype(BF)
    mix_ref[...] = lax.dot_general(weight, del_ref[...], (((0,), (0,)), ((), ())), preferred_element_type=F32)
    sent = mix_ref[own, :].astype(BF)
    for z in range(msg_ref.shape[0]):
        for b in range(nblk):
            msg_ref[z, b] = sent[:, b * BLK : (b + 1) * BLK]
    wg_ref[...] = lax.dot_general(
        del_ref[own, :], all_ref[...], (((1,), (1,)), ((), ())), preferred_element_type=F32
    )


def spread(got_ref, msg_ref, sems):
    copies = [pltpu.make_async_copy(got_ref, msg_ref.at[k], sems.at[k]) for k in range(msg_ref.shape[0])]
    for c in copies:
        c.start()
    for c in copies:
        c.wait()


def per_device(feats, weight, tile_values, tile_dest, tile_block, tile_source, cotangent):
    panel, rows = feats.shape
    tiles = tile_values.shape[0]
    nblk = rows // BLK
    ntot = NY * NZ * nblk
    near = NY * NP
    reps = NX * NC
    full = reps * panel
    rep = lax.axis_index(("x", "core")).astype(jnp.int32).reshape(1)
    shape = jax.ShapeDtypeStruct
    tile_scratch = [pltpu.VMEM((tiles, BLK, BLK), BF), pltpu.SemaphoreType.DMA((CHUNKS,))]
    tile_bytes = tiles * BLK * BLK * 2
    tile_flops = 2 * tiles * panel * BLK * BLK
    places = tuple(map(in_hbm, (tile_dest[:, 0], tile_block, tile_source)))
    tile_values = in_hbm(tile_values)

    parts = call(
        scatter_products,
        "scatter_products",
        pltpu.HBM((ntot, panel, BLK), BF),
        [SMEM, SMEM, SMEM, VMEM, HBM],
        [
            pltpu.VMEM((ntot, panel, BLK), F32),
            pltpu.VMEM((ntot, panel, BLK), BF),
            *tile_scratch,
            pltpu.SemaphoreType.DMA((CHUNKS,)),
        ],
        flops=tile_flops,
        nbytes=tile_bytes,
        outs=HBM,
    )(*places, in_hbm(feats), tile_values)

    got = lax.all_to_all(parts.reshape(near, NZ8 * nblk, panel, BLK), ("y", "zp"), 0, 0)
    both = lax.all_gather(
        jnp.concatenate([cotangent, weight.T], axis=1), ("x", "core"), axis=0, tiled=True
    )
    got, both = lax.optimization_barrier((got, both))
    half = call(sum_first, "sum_near", shape((NZ8 * nblk, panel, BLK), BF), [VMEM], nbytes=ntot * panel * BLK * 2)(got)
    got = lax.all_to_all(half.reshape(NZ8, nblk, panel, BLK), "z8", 0, 0)
    mine = call(finish_sum, "sum_far", shape((reps, nblk, panel, BLK), BF), [VMEM], nbytes=1 << 19)(got)
    gathered = lax.all_to_all(mine, ("x", "core"), 0, 0)

    hidden, sent, wgrad = call(
        middle,
        "middle",
        (
            shape((panel, rows), BF),
            shape((NZ8, nblk, panel, BLK), BF),
            shape((panel, full), F32),
        ),
        [SMEM, VMEM, VMEM],
        [pltpu.VMEM((full, rows), BF), pltpu.VMEM((full, rows), BF), pltpu.VMEM((full, rows), F32)],
        flops=6 * full * full * rows,
        nbytes=1 << 20,
    )(rep, gathered, both)

    col = lax.all_to_all(sent, "z8", 0, 0)
    wsum = jnp.sum(lax.all_gather(wgrad, "y", axis=0), axis=0)
    col, wsum = lax.optimization_barrier((col, wsum))
    copies = call(
        spread,
        "spread",
        pltpu.HBM((near, NZ8 * nblk, panel, BLK), BF),
        [VMEM],
        [pltpu.SemaphoreType.DMA((near,))],
        nbytes=ntot * panel * BLK * 2,
        outs=HBM,
    )(col.reshape(NZ8 * nblk, panel, BLK))
    every = lax.all_to_all(copies, ("y", "zp"), 0, 0)
    wsum = jnp.sum(lax.all_gather(wsum, ("z8", "zp"), axis=0), axis=0)
    weight_grad = (wsum * float(rows * NY * NZ) ** (-0.5)).T
    every, weight_grad = lax.optimization_barrier((every, weight_grad))

    input_grad = call(
        gather_products,
        "gather_products",
        shape((panel, rows), BF),
        [SMEM, SMEM, SMEM, VMEM, HBM],
        [pltpu.VMEM((nblk, panel, BLK), F32), *tile_scratch],
        flops=tile_flops,
        nbytes=tile_bytes,
    )(*places, every.reshape(ntot, panel, BLK), tile_values)
    return hidden, weight_grad, input_grad


def solution(mesh):
    split = Mesh(mesh.devices.reshape(NY, NZ8, NP, NX, NC), ("y", "z8", "zp", "x", "core"))
    dom, rep = ("y", "z8", "zp"), ("x", "core")
    placed = (P(rep, dom), P(None, rep), P(dom, None, None), P(dom, None), P(dom), P(dom), P(rep, dom))
    return jax.shard_map(
        per_device,
        mesh=split,
        in_specs=placed,
        out_specs=(P(rep, dom), P(None, rep), P(rep, dom)),
        check_vma=False,
    )
```

```python
import jax
import jax.numpy as jnp
from jax import lax
from jax.experimental import pallas as pl
from jax.experimental.pallas import tpu as pltpu
from jax.sharding import Mesh, PartitionSpec as P

BF = jnp.bfloat16
F32 = jnp.float32
NY, NZ, NX, NC = 4, 16, 4, 2
BLK = 128
CHUNKS = 8
NZ8, NP = NZ // 2, 2

SMEM = pl.BlockSpec(memory_space=pltpu.SMEM)
VMEM = pl.BlockSpec(memory_space=pltpu.VMEM)
HBM = pl.BlockSpec(memory_space=pltpu.HBM)


def in_hbm(x):
    return pltpu.with_memory_space_constraint(x, pltpu.HBM)


def slot(dest, block, nblk, stride):
    near = lax.shift_right_logical(dest, 4) * NP + (dest & (NP - 1))
    return near * stride + (lax.shift_right_logical(dest, 1) & (NZ8 - 1)) * nblk + block


def call(kernel, name, out_shape, in_specs, scratch=(), mib=24, flops=0, nbytes=0, outs=None):
    outs = outs or jax.tree.map(lambda _: VMEM, out_shape)
    return pl.pallas_call(
        kernel,
        name=name,
        out_shape=out_shape,
        in_specs=in_specs,
        out_specs=outs,
        scratch_shapes=list(scratch),
        compiler_params=pltpu.CompilerParams(vmem_limit_bytes=mib << 20),
        cost_estimate=pl.CostEstimate(flops=flops, bytes_accessed=nbytes, transcendentals=0),
    )


def tile_copies(tiles_ref, buf_ref, sems):
    n = tiles_ref.shape[0] // CHUNKS
    return [
        pltpu.make_async_copy(tiles_ref.at[pl.ds(c * n, n)], buf_ref.at[pl.ds(c * n, n)], sems.at[c])
        for c in range(CHUNKS)
    ]


def scatter_products(dest_ref, block_ref, src_ref, feats_ref, tiles_ref, out_ref, acc_ref, half_ref, buf_ref, sems, out_sems):
    copies = tile_copies(tiles_ref, buf_ref, sems)
    for c in copies:
        c.start()
    acc_ref[...] = jnp.zeros_like(acc_ref)
    n = tiles_ref.shape[0] // CHUNKS
    nblk = feats_ref.shape[1] // BLK
    for c in range(CHUNKS):
        copies[c].wait()
        for t in range(c * n, (c + 1) * n):
            col = pl.multiple_of(src_ref[t] * BLK, BLK)
            prod = lax.dot_general(
                feats_ref[:, pl.ds(col, BLK)],
                buf_ref[t],
                (((1,), (1,)), ((), ())),
                preferred_element_type=F32,
            )
            acc_ref[slot(dest_ref[t], block_ref[t], nblk, NZ8 * nblk)] += prod
    m = out_ref.shape[0] // CHUNKS
    writes = []
    for c in range(CHUNKS):
        part = pl.ds(c * m, m)
        half_ref[part] = acc_ref[part].astype(BF)
        writes.append(pltpu.make_async_copy(half_ref.at[part], out_ref.at[part], out_sems.at[c]))
        writes[c].start()
    for c in range(CHUNKS):
        writes[c].wait()


def gather_products(dest_ref, block_ref, src_ref, every_ref, tiles_ref, out_ref, wg_ref, acc_ref, buf_ref, sems):
    copies = tile_copies(tiles_ref, buf_ref, sems)
    for c in copies:
        c.start()
    acc_ref[...] = jnp.zeros_like(acc_ref)
    n = tiles_ref.shape[0] // CHUNKS
    nblk, panel, _ = acc_ref.shape
    stride = every_ref.shape[0] // (NY * NP)
    for h in range(stride - NZ8 * nblk):
        total = jnp.zeros((panel, BLK), F32)
        for k in range(NY * NP):
            total += every_ref[k * stride + NZ8 * nblk + h].astype(F32)
        wg_ref[:, h * BLK : (h + 1) * BLK] = total * float(nblk * BLK * NY * NZ) ** (-0.5)
    for c in range(CHUNKS):
        copies[c].wait()
        for t in range(c * n, (c + 1) * n):
            prod = jnp.dot(
                every_ref[slot(dest_ref[t], block_ref[t], nblk, stride)], buf_ref[t], preferred_element_type=F32
            )
            acc_ref[src_ref[t]] += prod
    for b in range(nblk):
        out_ref[:, b * BLK : (b + 1) * BLK] = acc_ref[b].astype(BF)


def sum_first(got_ref, out_ref):
    total = got_ref[0].astype(F32)
    for k in range(1, got_ref.shape[0]):
        total += got_ref[k].astype(F32)
    out_ref[...] = total.astype(BF)


def finish_sum(got_ref, out_ref):
    for b in range(got_ref.shape[1]):
        total = got_ref[0, b].astype(F32)
        for k in range(1, got_ref.shape[0]):
            total += got_ref[k, b].astype(F32)
        total = total.astype(BF)
        for r in range(out_ref.shape[0]):
            out_ref[r, b] = total


def middle(rep_ref, got_ref, both_ref, hid_ref, msg_ref, all_ref, del_ref, mix_ref):
    cores, chips, nblk, panel, _ = got_ref.shape
    rows = nblk * BLK
    for r in range(cores * chips):
        for b in range(nblk):
            all_ref[r * panel : (r + 1) * panel, b * BLK : (b + 1) * BLK] = got_ref[r % cores, r // cores, b]
    own = pl.ds(pl.multiple_of(rep_ref[0] * panel, panel), panel)
    weight = both_ref[:, rows:]
    mixed = jnp.dot(weight, all_ref[...], preferred_element_type=F32)
    mix_ref[...] = mixed
    sig = jax.nn.sigmoid(mixed)
    delta = both_ref[:, :rows].astype(F32) * sig * (1.0 + mixed * (1.0 - sig))
    del_ref[...] = delta.astype(BF)
    mine = mix_ref[own, :]
    hid_ref[...] = (mine * jax.nn.sigmoid(mine)).astype(BF)
    mix_ref[...] = lax.dot_general(weight, del_ref[...], (((0,), (0,)), ((), ())), preferred_element_type=F32)
    sent = mix_ref[own, :].astype(BF)
    wgrad = lax.dot_general(
        del_ref[own, :], all_ref[...], (((1,), (1,)), ((), ())), preferred_element_type=F32
    ).astype(BF)
    for z in range(msg_ref.shape[0]):
        for b in range(nblk):
            msg_ref[z, b] = sent[:, b * BLK : (b + 1) * BLK]
        for h in range(msg_ref.shape[1] - nblk):
            msg_ref[z, nblk + h] = wgrad[:, h * BLK : (h + 1) * BLK]


def spread(got_ref, msg_ref, one_ref, sems):
    pairs, blocks, panel, _ = got_ref.shape
    nblk = (one_ref.shape[0] - blocks) // (pairs - 1)
    for z in range(pairs):
        one_ref[z * nblk : (z + 1) * nblk] = got_ref[z, :nblk]
    for h in range(blocks - nblk):
        total = jnp.zeros((panel, BLK), F32)
        for z in range(pairs):
            total += got_ref[z, nblk + h].astype(F32)
        one_ref[pairs * nblk + h] = total.astype(BF)
    copies = [pltpu.make_async_copy(one_ref, msg_ref.at[k], sems.at[k]) for k in range(msg_ref.shape[0])]
    for c in copies:
        c.start()
    for c in copies:
        c.wait()


def per_device(feats, weight, tile_values, tile_dest, tile_block, tile_source, cotangent):
    panel, rows = feats.shape
    tiles = tile_values.shape[0]
    nblk = rows // BLK
    ntot = NY * NZ * nblk
    near = NY * NP
    full = NX * NC * panel
    halves = full // BLK
    stride = NZ8 * nblk + halves
    rep = lax.axis_index(("x", "core")).astype(jnp.int32).reshape(1)
    shape = jax.ShapeDtypeStruct
    tile_scratch = [pltpu.VMEM((tiles, BLK, BLK), BF), pltpu.SemaphoreType.DMA((CHUNKS,))]
    tile_bytes = tiles * BLK * BLK * 2
    tile_flops = 2 * tiles * panel * BLK * BLK
    places = tuple(map(in_hbm, (tile_dest[:, 0], tile_block, tile_source)))
    tile_values = in_hbm(tile_values)

    parts = call(
        scatter_products,
        "scatter_products",
        pltpu.HBM((ntot, panel, BLK), BF),
        [SMEM, SMEM, SMEM, VMEM, HBM],
        [
            pltpu.VMEM((ntot, panel, BLK), F32),
            pltpu.VMEM((ntot, panel, BLK), BF),
            *tile_scratch,
            pltpu.SemaphoreType.DMA((CHUNKS,)),
        ],
        flops=tile_flops,
        nbytes=tile_bytes,
        outs=HBM,
    )(*places, in_hbm(feats), tile_values)

    got = lax.all_to_all(parts.reshape(near, NZ8 * nblk, panel, BLK), ("y", "zp"), 0, 0)
    both = lax.all_gather(
        jnp.concatenate([cotangent, weight.T], axis=1), ("x", "core"), axis=0, tiled=True
    )
    got, both = lax.optimization_barrier((got, both))
    half = call(sum_first, "sum_near", shape((NZ8 * nblk, panel, BLK), BF), [VMEM], nbytes=ntot * panel * BLK * 2)(got)
    got = lax.all_to_all(half.reshape(NZ8, nblk, panel, BLK), "z8", 0, 0)
    mine = call(finish_sum, "sum_far", shape((NX, nblk, panel, BLK), BF), [VMEM], nbytes=1 << 19)(got)
    gathered = lax.all_gather(lax.all_to_all(mine, "x", 0, 0), "core", axis=0)

    hidden, sent = call(
        middle,
        "middle",
        (
            shape((panel, rows), BF),
            shape((NZ8, nblk + halves, panel, BLK), BF),
        ),
        [SMEM, VMEM, VMEM],
        [pltpu.VMEM((full, rows), BF), pltpu.VMEM((full, rows), BF), pltpu.VMEM((full, rows), F32)],
        flops=6 * full * full * rows,
        nbytes=1 << 20,
    )(rep, gathered, both)

    col = lax.all_to_all(sent, "z8", 0, 0)
    copies = call(
        spread,
        "spread",
        pltpu.HBM((near, stride, panel, BLK), BF),
        [VMEM],
        [pltpu.VMEM((stride, panel, BLK), BF), pltpu.SemaphoreType.DMA((near,))],
        nbytes=ntot * panel * BLK * 2,
        outs=HBM,
    )(col)
    every = lax.all_to_all(copies, ("y", "zp"), 0, 0)

    input_grad, weight_grad = call(
        gather_products,
        "gather_products",
        (shape((panel, rows), BF), shape((panel, full), F32)),
        [SMEM, SMEM, SMEM, VMEM, HBM],
        [pltpu.VMEM((nblk, panel, BLK), F32), *tile_scratch],
        flops=tile_flops,
        nbytes=tile_bytes,
    )(*places, every.reshape(near * stride, panel, BLK), tile_values)
    return hidden, weight_grad.T, input_grad


def solution(mesh):
    split = Mesh(mesh.devices.reshape(NY, NZ8, NP, NX, NC), ("y", "z8", "zp", "x", "core"))
    dom, rep = ("y", "z8", "zp"), ("x", "core")
    placed = (P(rep, dom), P(None, rep), P(dom, None, None), P(dom, None), P(dom), P(dom), P(rep, dom))
    return jax.shard_map(
        per_device,
        mesh=split,
        in_specs=placed,
        out_specs=(P(rep, dom), P(None, rep), P(rep, dom)),
        check_vma=False,
    )
```

```python
import math

import jax
import jax.numpy as jnp
import numpy as np
from jax import lax
from jax.experimental import pallas as pl
from jax.experimental.pallas import tpu as pltpu
from jax.sharding import Mesh, PartitionSpec as P

BF = jnp.bfloat16
F32 = jnp.float32
NY, NZ, NX, NC = 4, 16, 4, 2
BLK = 128
CHUNKS = (16, 48, 64)
WRITES = 4
NZ8, NP = NZ // 2, 2

SMEM = pl.BlockSpec(memory_space=pltpu.SMEM)
VMEM = pl.BlockSpec(memory_space=pltpu.VMEM)
HBM = pl.BlockSpec(memory_space=pltpu.HBM)


def in_hbm(x):
    return pltpu.with_memory_space_constraint(x, pltpu.HBM)


AXES = ("y", "z8", "zp", "x", "core")
SIZES = (NY, NZ8, NP, NX, NC)
NEAR_ORDER = [(0, 0), (1, 0), (2, 0), (3, 0), (0, 1), (1, 1), (2, 1), (3, 1)]
FAR_ORDER = [(0,), (4,), (2,), (6,), (1,), (5,), (3,), (7,)]
X_ORDER = [(0,), (2,), (1,), (3,)]


def exchange(x, axes, order):
    others = [a for a in AXES if a not in axes]
    ranks = np.arange(math.prod(SIZES)).reshape(SIZES)
    ranks = ranks.transpose([AXES.index(a) for a in (*others, *axes)])
    ranks = ranks.reshape(-1, *(SIZES[AXES.index(a)] for a in axes))
    groups = [[int(r[m]) for m in order] for r in ranks]
    flat = x.reshape(x.shape[0], -1, BLK)
    return lax.all_to_all(flat, AXES, 0, 0, tiled=True, axis_index_groups=groups).reshape(x.shape)


def slot(dest, block, nblk, stride):
    y, z = lax.shift_right_logical(dest, 4), dest & 15
    near = (z & 1) * 4 + y
    far = (z & 2) * 2 + lax.shift_right_logical(z & 4, 1) + lax.shift_right_logical(z, 3)
    return near * stride + far * nblk + block


def call(kernel, name, out_shape, in_specs, scratch=(), mib=24, flops=0, nbytes=0, outs=None):
    outs = outs or jax.tree.map(lambda _: VMEM, out_shape)
    return pl.pallas_call(
        kernel,
        name=name,
        out_shape=out_shape,
        in_specs=in_specs,
        out_specs=outs,
        scratch_shapes=list(scratch),
        compiler_params=pltpu.CompilerParams(vmem_limit_bytes=mib << 20),
        cost_estimate=pl.CostEstimate(flops=flops, bytes_accessed=nbytes, transcendentals=0),
    )


def scatter_products(
    dest_ref, block_ref, src_ref, feats_ref, tiles_ref, out_ref, acc_ref, half_ref, buf_ref, sems, out_sems
):
    copies = []
    for c, n in enumerate(CHUNKS):
        part = pl.ds(sum(CHUNKS[:c]), n)
        copies.append(pltpu.make_async_copy(tiles_ref.at[part], buf_ref.at[part], sems.at[c]))
        copies[c].start()
    acc_ref[...] = jnp.zeros_like(acc_ref)
    nblk = feats_ref.shape[1] // BLK
    for c, n in enumerate(CHUNKS):
        copies[c].wait()
        for t in range(sum(CHUNKS[:c]), sum(CHUNKS[:c]) + n):
            col = pl.multiple_of(src_ref[t] * BLK, BLK)
            prod = lax.dot_general(
                feats_ref[:, pl.ds(col, BLK)],
                buf_ref[t],
                (((1,), (1,)), ((), ())),
                preferred_element_type=F32,
            )
            acc_ref[slot(dest_ref[t], block_ref[t], nblk, NZ8 * nblk)] += prod
    m = out_ref.shape[0] // WRITES
    writes = []
    for c in range(WRITES):
        part = pl.ds(c * m, m)
        half_ref[part] = acc_ref[part].astype(BF)
        writes.append(pltpu.make_async_copy(half_ref.at[part], out_ref.at[part], out_sems.at[c]))
        writes[c].start()
    for c in range(WRITES):
        writes[c].wait()


def gather_products(dest_ref, block_ref, src_ref, every_ref, tiles_ref, out_ref, wg_ref, acc_ref):
    acc_ref[...] = jnp.zeros_like(acc_ref)
    nblk, panel, _ = acc_ref.shape
    stride = every_ref.shape[0] // (NY * NP)
    for h in range(stride - NZ8 * nblk):
        total = jnp.zeros((panel, BLK), F32)
        for k in range(NY * NP):
            total += every_ref[k * stride + NZ8 * nblk + h].astype(F32)
        wg_ref[:, h * BLK : (h + 1) * BLK] = total * float(nblk * BLK * NY * NZ) ** (-0.5)
    for t in range(tiles_ref.shape[0]):
        prod = jnp.dot(
            every_ref[slot(dest_ref[t], block_ref[t], nblk, stride)], tiles_ref[t], preferred_element_type=F32
        )
        acc_ref[src_ref[t]] += prod
    for b in range(nblk):
        out_ref[:, b * BLK : (b + 1) * BLK] = acc_ref[b].astype(BF)


def sum_first(got_ref, out_ref):
    total = got_ref[0].astype(F32)
    for k in range(1, got_ref.shape[0]):
        total += got_ref[k].astype(F32)
    out_ref[...] = total.astype(BF)


def finish_sum(got_ref, out_ref):
    for b in range(got_ref.shape[1]):
        total = got_ref[0, b].astype(F32)
        for k in range(1, got_ref.shape[0]):
            total += got_ref[k, b].astype(F32)
        total = total.astype(BF)
        for r in range(out_ref.shape[0]):
            out_ref[r, b] = total


def middle(rep_ref, got_ref, both_ref, hid_ref, msg_ref, all_ref, del_ref, mix_ref):
    cores, chips, nblk, panel, _ = got_ref.shape
    rows = nblk * BLK
    for r in range(cores * chips):
        for b in range(nblk):
            all_ref[r * panel : (r + 1) * panel, b * BLK : (b + 1) * BLK] = got_ref[r % cores, [m[0] for m in X_ORDER].index(r // cores), b]
    own = pl.ds(pl.multiple_of(rep_ref[0] * panel, panel), panel)
    weight = both_ref[:, rows:]
    mixed = jnp.dot(weight, all_ref[...], preferred_element_type=F32)
    mix_ref[...] = mixed
    sig = jax.nn.sigmoid(mixed)
    delta = both_ref[:, :rows].astype(F32) * sig * (1.0 + mixed * (1.0 - sig))
    del_ref[...] = delta.astype(BF)
    mine = mix_ref[own, :]
    hid_ref[...] = (mine * jax.nn.sigmoid(mine)).astype(BF)
    mix_ref[...] = lax.dot_general(weight, del_ref[...], (((0,), (0,)), ((), ())), preferred_element_type=F32)
    sent = mix_ref[own, :].astype(BF)
    wgrad = lax.dot_general(
        del_ref[own, :], all_ref[...], (((1,), (1,)), ((), ())), preferred_element_type=F32
    ).astype(BF)
    for z in range(msg_ref.shape[0]):
        for b in range(nblk):
            msg_ref[z, b] = sent[:, b * BLK : (b + 1) * BLK]
        for h in range(msg_ref.shape[1] - nblk):
            msg_ref[z, nblk + h] = wgrad[:, h * BLK : (h + 1) * BLK]


def spread(got_ref, msg_ref, one_ref, sems):
    pairs, blocks, panel, _ = got_ref.shape
    nblk = (one_ref.shape[0] - blocks) // (pairs - 1)
    for z in range(pairs):
        one_ref[z * nblk : (z + 1) * nblk] = got_ref[z, :nblk]
    for h in range(blocks - nblk):
        total = jnp.zeros((panel, BLK), F32)
        for z in range(pairs):
            total += got_ref[z, nblk + h].astype(F32)
        one_ref[pairs * nblk + h] = total.astype(BF)
    copies = [pltpu.make_async_copy(one_ref, msg_ref.at[k], sems.at[k]) for k in range(msg_ref.shape[0])]
    for c in copies:
        c.start()
    for c in copies:
        c.wait()


def per_device(feats, weight, tile_values, tile_dest, tile_block, tile_source, cotangent):
    panel, rows = feats.shape
    tiles = tile_values.shape[0]
    nblk = rows // BLK
    ntot = NY * NZ * nblk
    near = NY * NP
    full = NX * NC * panel
    halves = full // BLK
    stride = NZ8 * nblk + halves
    rep = lax.axis_index(("x", "core")).astype(jnp.int32).reshape(1)
    shape = jax.ShapeDtypeStruct
    tile_bytes = tiles * BLK * BLK * 2
    tile_flops = 2 * tiles * panel * BLK * BLK
    places = tuple(map(in_hbm, (tile_dest[:, 0], tile_block, tile_source)))

    parts = call(
        scatter_products,
        "scatter_products",
        pltpu.HBM((ntot, panel, BLK), BF),
        [SMEM, SMEM, SMEM, VMEM, HBM],
        [
            pltpu.VMEM((ntot, panel, BLK), F32),
            pltpu.VMEM((ntot, panel, BLK), BF),
            pltpu.VMEM((tiles, BLK, BLK), BF),
            pltpu.SemaphoreType.DMA((len(CHUNKS),)),
            pltpu.SemaphoreType.DMA((WRITES,)),
        ],
        flops=tile_flops,
        nbytes=tile_bytes,
        outs=HBM,
    )(*places, in_hbm(feats), in_hbm(tile_values))

    got = exchange(parts.reshape(near, NZ8 * nblk, panel, BLK), ("y", "zp"), NEAR_ORDER)
    both = lax.all_gather(
        jnp.concatenate([cotangent, weight.T], axis=1), ("x", "core"), axis=0, tiled=True
    )
    got, both = lax.optimization_barrier((got, both))
    half = call(sum_first, "sum_near", shape((NZ8 * nblk, panel, BLK), BF), [VMEM], nbytes=ntot * panel * BLK * 2)(got)
    got = exchange(half.reshape(NZ8, nblk, panel, BLK), ("z8",), FAR_ORDER)
    mine = call(finish_sum, "sum_far", shape((NX, nblk, panel, BLK), BF), [VMEM], nbytes=1 << 19)(got)
    gathered = lax.all_gather(exchange(mine, ("x",), X_ORDER), "core", axis=0)

    hidden, sent = call(
        middle,
        "middle",
        (
            shape((panel, rows), BF),
            shape((NZ8, nblk + halves, panel, BLK), BF),
        ),
        [SMEM, VMEM, VMEM],
        [pltpu.VMEM((full, rows), BF), pltpu.VMEM((full, rows), BF), pltpu.VMEM((full, rows), F32)],
        flops=6 * full * full * rows,
        nbytes=1 << 20,
    )(rep, gathered, both)

    col = exchange(sent, ("z8",), FAR_ORDER)
    copies = call(
        spread,
        "spread",
        pltpu.HBM((near, stride, panel, BLK), BF),
        [VMEM],
        [pltpu.VMEM((stride, panel, BLK), BF), pltpu.SemaphoreType.DMA((near,))],
        nbytes=ntot * panel * BLK * 2,
        outs=HBM,
    )(col)
    every = exchange(copies, ("y", "zp"), NEAR_ORDER)

    input_grad, weight_grad = call(
        gather_products,
        "gather_products",
        (shape((panel, rows), BF), shape((panel, full), F32)),
        [SMEM, SMEM, SMEM, VMEM, VMEM],
        [pltpu.VMEM((nblk, panel, BLK), F32)],
        flops=tile_flops,
        nbytes=tile_bytes,
    )(*places, every.reshape(near * stride, panel, BLK), tile_values)
    return hidden, weight_grad.T, input_grad


def solution(mesh):
    split = Mesh(mesh.devices.reshape(NY, NZ8, NP, NX, NC), ("y", "z8", "zp", "x", "core"))
    dom, rep = ("y", "z8", "zp"), ("x", "core")
    placed = (P(rep, dom), P(None, rep), P(dom, None, None), P(dom, None), P(dom), P(dom), P(rep, dom))
    return jax.shard_map(
        per_device,
        mesh=split,
        in_specs=placed,
        out_specs=(P(rep, dom), P(None, rep), P(rep, dom)),
        check_vma=False,
    )
```

```python
import math

import jax
import jax.numpy as jnp
import numpy as np
from jax import lax
from jax.experimental import pallas as pl
from jax.experimental.pallas import tpu as pltpu
from jax.sharding import Mesh, PartitionSpec as P

BF = jnp.bfloat16
F32 = jnp.float32
NY, NZ, NX, NC = 4, 16, 4, 2
BLK = 128
CHUNKS = (16, 48, 64)
WRITES = 4
NZ8, NP = NZ // 2, 2

SMEM = pl.BlockSpec(memory_space=pltpu.SMEM)
VMEM = pl.BlockSpec(memory_space=pltpu.VMEM)
HBM = pl.BlockSpec(memory_space=pltpu.HBM)


def in_hbm(x):
    return pltpu.with_memory_space_constraint(x, pltpu.HBM)


AXES = ("y", "z8", "zp", "x", "core")
SIZES = (NY, NZ8, NP, NX, NC)
NEAR_ORDER = [(0, 0), (1, 0), (2, 0), (3, 0), (0, 1), (1, 1), (2, 1), (3, 1)]
FAR_ORDER = [(0,), (4,), (2,), (6,), (1,), (5,), (3,), (7,)]
NEAR_TURN, FAR_TURN = 4, 7
X_ORDER = [(0,), (2,), (1,), (3,)]


def exchange(x, axes, order, turn=0):
    others = [a for a in AXES if a not in axes]
    ranks = np.arange(math.prod(SIZES)).reshape(SIZES)
    ranks = ranks.transpose([AXES.index(a) for a in (*others, *axes)])
    ranks = ranks.reshape(-1, *(SIZES[AXES.index(a)] for a in axes))
    groups = [[int(r[order[i ^ (turn * (r.flat[0] % NC))]]) for i in range(len(order))] for r in ranks]
    flat = x.reshape(x.shape[0], -1, BLK)
    return lax.all_to_all(flat, AXES, 0, 0, tiled=True, axis_index_groups=groups).reshape(x.shape)


def slot(dest, block, core, nblk, stride):
    y, z = lax.shift_right_logical(dest, 4), dest & 15
    near = ((z & 1) * 4 + y) ^ (core * NEAR_TURN)
    far = ((z & 2) * 2 + lax.shift_right_logical(z & 4, 1) + lax.shift_right_logical(z, 3)) ^ (core * FAR_TURN)
    return near * stride + far * nblk + block


def call(kernel, name, out_shape, in_specs, scratch=(), mib=24, flops=0, nbytes=0, outs=None):
    outs = outs or jax.tree.map(lambda _: VMEM, out_shape)
    return pl.pallas_call(
        kernel,
        name=name,
        out_shape=out_shape,
        in_specs=in_specs,
        out_specs=outs,
        scratch_shapes=list(scratch),
        compiler_params=pltpu.CompilerParams(vmem_limit_bytes=mib << 20),
        cost_estimate=pl.CostEstimate(flops=flops, bytes_accessed=nbytes, transcendentals=0),
    )


def scatter_products(
    core_ref, dest_ref, block_ref, src_ref, feats_ref, tiles_ref, out_ref, acc_ref, half_ref, buf_ref, sems, out_sems
):
    copies = []
    for c, n in enumerate(CHUNKS):
        part = pl.ds(sum(CHUNKS[:c]), n)
        copies.append(pltpu.make_async_copy(tiles_ref.at[part], buf_ref.at[part], sems.at[c]))
        copies[c].start()
    acc_ref[...] = jnp.zeros_like(acc_ref)
    nblk = feats_ref.shape[1] // BLK
    for c, n in enumerate(CHUNKS):
        copies[c].wait()
        for t in range(sum(CHUNKS[:c]), sum(CHUNKS[:c]) + n):
            col = pl.multiple_of(src_ref[t] * BLK, BLK)
            prod = lax.dot_general(
                feats_ref[:, pl.ds(col, BLK)],
                buf_ref[t],
                (((1,), (1,)), ((), ())),
                preferred_element_type=F32,
            )
            acc_ref[slot(dest_ref[t], block_ref[t], core_ref[0], nblk, NZ8 * nblk)] += prod
    m = out_ref.shape[0] // WRITES
    writes = []
    for c in range(WRITES):
        part = pl.ds(c * m, m)
        half_ref[part] = acc_ref[part].astype(BF)
        writes.append(pltpu.make_async_copy(half_ref.at[part], out_ref.at[part], out_sems.at[c]))
        writes[c].start()
    for c in range(WRITES):
        writes[c].wait()


def gather_products(core_ref, dest_ref, block_ref, src_ref, every_ref, tiles_ref, out_ref, wg_ref, acc_ref):
    acc_ref[...] = jnp.zeros_like(acc_ref)
    nblk, panel, _ = acc_ref.shape
    stride = every_ref.shape[0] // (NY * NP)
    for h in range(stride - NZ8 * nblk):
        total = jnp.zeros((panel, BLK), F32)
        for k in range(NY * NP):
            total += every_ref[k * stride + NZ8 * nblk + h].astype(F32)
        wg_ref[:, h * BLK : (h + 1) * BLK] = total * float(nblk * BLK * NY * NZ) ** (-0.5)
    for t in range(tiles_ref.shape[0]):
        prod = jnp.dot(
            every_ref[slot(dest_ref[t], block_ref[t], core_ref[0], nblk, stride)], tiles_ref[t], preferred_element_type=F32
        )
        acc_ref[src_ref[t]] += prod
    for b in range(nblk):
        out_ref[:, b * BLK : (b + 1) * BLK] = acc_ref[b].astype(BF)


def sum_first(got_ref, out_ref):
    total = got_ref[0].astype(F32)
    for k in range(1, got_ref.shape[0]):
        total += got_ref[k].astype(F32)
    out_ref[...] = total.astype(BF)


def finish_sum(got_ref, out_ref):
    for b in range(got_ref.shape[1]):
        total = got_ref[0, b].astype(F32)
        for k in range(1, got_ref.shape[0]):
            total += got_ref[k, b].astype(F32)
        total = total.astype(BF)
        for r in range(out_ref.shape[0]):
            out_ref[r, b] = total


def middle(rep_ref, got_ref, both_ref, hid_ref, msg_ref, all_ref, del_ref, mix_ref):
    cores, chips, nblk, panel, _ = got_ref.shape
    rows = nblk * BLK
    for r in range(cores * chips):
        for b in range(nblk):
            all_ref[r * panel : (r + 1) * panel, b * BLK : (b + 1) * BLK] = got_ref[r % cores, [m[0] for m in X_ORDER].index(r // cores), b]
    own = pl.ds(pl.multiple_of(rep_ref[0] * panel, panel), panel)
    weight = both_ref[:, rows:]
    mixed = jnp.dot(weight, all_ref[...], preferred_element_type=F32)
    mix_ref[...] = mixed
    sig = jax.nn.sigmoid(mixed)
    delta = both_ref[:, :rows].astype(F32) * sig * (1.0 + mixed * (1.0 - sig))
    del_ref[...] = delta.astype(BF)
    mine = mix_ref[own, :]
    hid_ref[...] = (mine * jax.nn.sigmoid(mine)).astype(BF)
    mix_ref[...] = lax.dot_general(weight, del_ref[...], (((0,), (0,)), ((), ())), preferred_element_type=F32)
    sent = mix_ref[own, :].astype(BF)
    wgrad = lax.dot_general(
        del_ref[own, :], all_ref[...], (((1,), (1,)), ((), ())), preferred_element_type=F32
    ).astype(BF)
    for z in range(msg_ref.shape[0]):
        for b in range(nblk):
            msg_ref[z, b] = sent[:, b * BLK : (b + 1) * BLK]
        for h in range(msg_ref.shape[1] - nblk):
            msg_ref[z, nblk + h] = wgrad[:, h * BLK : (h + 1) * BLK]


def spread(got_ref, msg_ref):
    pairs, blocks, panel, _ = got_ref.shape
    near, stride = msg_ref.shape[:2]
    nblk = (stride - blocks) // (pairs - 1)
    for h in range(blocks - nblk):
        total = jnp.zeros((panel, BLK), F32)
        for z in range(pairs):
            total += got_ref[z, nblk + h].astype(F32)
        for k in range(near):
            msg_ref[k, pairs * nblk + h] = total.astype(BF)
    for z in range(pairs):
        one = got_ref[z, :nblk]
        for k in range(near):
            msg_ref[k, z * nblk : (z + 1) * nblk] = one


def per_device(feats, weight, tile_values, tile_dest, tile_block, tile_source, cotangent):
    panel, rows = feats.shape
    tiles = tile_values.shape[0]
    nblk = rows // BLK
    ntot = NY * NZ * nblk
    near = NY * NP
    full = NX * NC * panel
    halves = full // BLK
    stride = NZ8 * nblk + halves
    rep = lax.axis_index(("x", "core")).astype(jnp.int32).reshape(1)
    shape = jax.ShapeDtypeStruct
    tile_bytes = tiles * BLK * BLK * 2
    tile_flops = 2 * tiles * panel * BLK * BLK
    core = lax.axis_index("core").astype(jnp.int32).reshape(1)
    places = (core, *map(in_hbm, (tile_dest[:, 0], tile_block, tile_source)))

    parts = call(
        scatter_products,
        "scatter_products",
        pltpu.HBM((ntot, panel, BLK), BF),
        [SMEM, SMEM, SMEM, SMEM, VMEM, HBM],
        [
            pltpu.VMEM((ntot, panel, BLK), F32),
            pltpu.VMEM((ntot, panel, BLK), BF),
            pltpu.VMEM((tiles, BLK, BLK), BF),
            pltpu.SemaphoreType.DMA((len(CHUNKS),)),
            pltpu.SemaphoreType.DMA((WRITES,)),
        ],
        flops=tile_flops,
        nbytes=tile_bytes,
        outs=HBM,
    )(*places, in_hbm(feats), in_hbm(tile_values))

    got = exchange(parts.reshape(near, NZ8 * nblk, panel, BLK), ("y", "zp"), NEAR_ORDER, NEAR_TURN)
    both = lax.all_gather(
        jnp.concatenate([cotangent, weight.T], axis=1), ("x", "core"), axis=0, tiled=True
    )
    got, both = lax.optimization_barrier((got, both))
    half = call(sum_first, "sum_near", shape((NZ8 * nblk, panel, BLK), BF), [VMEM], nbytes=ntot * panel * BLK * 2)(got)
    got = exchange(half.reshape(NZ8, nblk, panel, BLK), ("z8",), FAR_ORDER, FAR_TURN)
    mine = call(finish_sum, "sum_far", shape((NX, nblk, panel, BLK), BF), [VMEM], nbytes=1 << 19)(got)
    gathered = lax.all_gather(exchange(mine, ("x",), X_ORDER), "core", axis=0)

    hidden, sent = call(
        middle,
        "middle",
        (
            shape((panel, rows), BF),
            shape((NZ8, nblk + halves, panel, BLK), BF),
        ),
        [SMEM, VMEM, VMEM],
        [pltpu.VMEM((full, rows), BF), pltpu.VMEM((full, rows), BF), pltpu.VMEM((full, rows), F32)],
        flops=6 * full * full * rows,
        nbytes=1 << 20,
    )(rep, gathered, both)

    col = exchange(sent, ("z8",), FAR_ORDER, FAR_TURN)
    copies = call(
        spread,
        "spread",
        shape((near, stride, panel, BLK), BF),
        [VMEM],
        nbytes=ntot * panel * BLK * 2,
    )(col)
    every = exchange(copies, ("y", "zp"), NEAR_ORDER, NEAR_TURN)

    input_grad, weight_grad = call(
        gather_products,
        "gather_products",
        (shape((panel, rows), BF), shape((panel, full), F32)),
        [SMEM, SMEM, SMEM, SMEM, VMEM, VMEM],
        [pltpu.VMEM((nblk, panel, BLK), F32)],
        flops=tile_flops,
        nbytes=tile_bytes,
    )(*places, every.reshape(near * stride, panel, BLK), tile_values)
    return hidden, weight_grad.T, input_grad


def solution(mesh):
    split = Mesh(mesh.devices.reshape(NY, NZ8, NP, NX, NC), ("y", "z8", "zp", "x", "core"))
    dom, rep = ("y", "z8", "zp"), ("x", "core")
    placed = (P(rep, dom), P(None, rep), P(dom, None, None), P(dom, None), P(dom), P(dom), P(rep, dom))
    return jax.shard_map(
        per_device,
        mesh=split,
        in_specs=placed,
        out_specs=(P(rep, dom), P(None, rep), P(rep, dom)),
        check_vma=False,
    )
```

```python
import math

import jax
import jax.numpy as jnp
import numpy as np
from jax import lax
from jax.experimental import pallas as pl
from jax.experimental.pallas import tpu as pltpu
from jax.sharding import Mesh, PartitionSpec as P

BF = jnp.bfloat16
F32 = jnp.float32
NY, NZ, NX, NC = 4, 16, 4, 2
BLK = 128
CHUNKS = (16, 48, 64)
WRITES = 4
NZ8, NP = NZ // 2, 2

SMEM = pl.BlockSpec(memory_space=pltpu.SMEM)
VMEM = pl.BlockSpec(memory_space=pltpu.VMEM)
HBM = pl.BlockSpec(memory_space=pltpu.HBM)


def in_hbm(x):
    return pltpu.with_memory_space_constraint(x, pltpu.HBM)


AXES = ("y", "z8", "zp", "x", "core")
SIZES = (NY, NZ8, NP, NX, NC)
NEAR_ORDER = [(0, 0), (1, 0), (2, 0), (3, 0), (0, 1), (1, 1), (2, 1), (3, 1)]
FAR_ORDER = [(0,), (4,), (2,), (6,), (1,), (5,), (3,), (7,)]
NEAR_TURN, FAR_TURN = 4, 7
X_ORDER = [(0,), (2,), (1,), (3,)]


def exchange(x, axes, order, turn=0):
    others = [a for a in AXES if a not in axes]
    ranks = np.arange(math.prod(SIZES)).reshape(SIZES)
    ranks = ranks.transpose([AXES.index(a) for a in (*others, *axes)])
    ranks = ranks.reshape(-1, *(SIZES[AXES.index(a)] for a in axes))
    groups = [[int(r[order[i ^ (turn * (r.flat[0] % NC))]]) for i in range(len(order))] for r in ranks]
    flat = x.reshape(x.shape[0], -1, BLK)
    return lax.all_to_all(flat, AXES, 0, 0, tiled=True, axis_index_groups=groups).reshape(x.shape)


def slot(dest, block, core, nblk, stride):
    y, z = lax.shift_right_logical(dest, 4), dest & 15
    near = ((z & 1) * 4 + y) ^ (core * NEAR_TURN)
    far = ((z & 2) * 2 + lax.shift_right_logical(z & 4, 1) + lax.shift_right_logical(z, 3)) ^ (core * FAR_TURN)
    return near * stride + far * nblk + block


def call(kernel, name, out_shape, in_specs, scratch=(), mib=24, flops=0, nbytes=0, outs=None):
    outs = outs or jax.tree.map(lambda _: VMEM, out_shape)
    return pl.pallas_call(
        kernel,
        name=name,
        out_shape=out_shape,
        in_specs=in_specs,
        out_specs=outs,
        scratch_shapes=list(scratch),
        compiler_params=pltpu.CompilerParams(vmem_limit_bytes=mib << 20),
        cost_estimate=pl.CostEstimate(flops=flops, bytes_accessed=nbytes, transcendentals=0),
    )


def scatter_products(
    rep_ref, dest_ref, block_ref, src_ref, feats_ref, tiles_ref, out_ref, acc_ref, half_ref, buf_ref, sems, out_sems
):
    copies = []
    for c, n in enumerate(CHUNKS):
        part = pl.ds(sum(CHUNKS[:c]), n)
        copies.append(pltpu.make_async_copy(tiles_ref.at[part], buf_ref.at[part], sems.at[c]))
        copies[c].start()
    acc_ref[...] = jnp.zeros_like(acc_ref)
    nblk = feats_ref.shape[1] // BLK
    for c, n in enumerate(CHUNKS):
        copies[c].wait()
        for t in range(sum(CHUNKS[:c]), sum(CHUNKS[:c]) + n):
            col = pl.multiple_of(src_ref[t] * BLK, BLK)
            prod = lax.dot_general(
                feats_ref[:, pl.ds(col, BLK)],
                buf_ref[t],
                (((1,), (1,)), ((), ())),
                preferred_element_type=F32,
            )
            acc_ref[slot(dest_ref[t], block_ref[t], rep_ref[0] & 1, nblk, NZ8 * nblk)] += prod
    m = out_ref.shape[0] // WRITES
    writes = []
    for c in range(WRITES):
        part = pl.ds(c * m, m)
        half_ref[part] = acc_ref[part].astype(BF)
        writes.append(pltpu.make_async_copy(half_ref.at[part], out_ref.at[part], out_sems.at[c]))
        writes[c].start()
    for c in range(WRITES):
        writes[c].wait()


def gather_products(rep_ref, dest_ref, block_ref, src_ref, every_ref, tiles_ref, out_ref, wg_ref, acc_ref):
    acc_ref[...] = jnp.zeros_like(acc_ref)
    nblk, panel, _ = acc_ref.shape
    stride = every_ref.shape[0] // (NY * NP)
    for h in range(stride - NZ8 * nblk):
        total = jnp.zeros((panel, BLK), F32)
        for k in range(NY * NP):
            total += every_ref[k * stride + NZ8 * nblk + h].astype(F32)
        wg_ref[:, h * BLK : (h + 1) * BLK] = total * float(nblk * BLK * NY * NZ) ** (-0.5)
    for t in range(tiles_ref.shape[0]):
        prod = jnp.dot(
            every_ref[slot(dest_ref[t], block_ref[t], rep_ref[0] & 1, nblk, stride)], tiles_ref[t], preferred_element_type=F32
        )
        acc_ref[src_ref[t]] += prod
    for b in range(nblk):
        out_ref[:, b * BLK : (b + 1) * BLK] = acc_ref[b].astype(BF)


def sum_first(got_ref, out_ref):
    total = got_ref[0].astype(F32)
    for k in range(1, got_ref.shape[0]):
        total += got_ref[k].astype(F32)
    out_ref[...] = total.astype(BF)


def finish_sum(got_ref, out_ref):
    for b in range(got_ref.shape[1]):
        total = got_ref[0, b].astype(F32)
        for k in range(1, got_ref.shape[0]):
            total += got_ref[k, b].astype(F32)
        total = total.astype(BF)
        for r in range(out_ref.shape[0]):
            out_ref[r, b] = total


def middle(rep_ref, got_ref, both_ref, hid_ref, msg_ref, all_ref, del_ref, mix_ref):
    cores, chips, nblk, panel, _ = got_ref.shape
    rows = nblk * BLK
    for r in range(cores * chips):
        for b in range(nblk):
            all_ref[r * panel : (r + 1) * panel, b * BLK : (b + 1) * BLK] = got_ref[r % cores, [m[0] for m in X_ORDER].index(r // cores), b]
    own = pl.ds(pl.multiple_of(rep_ref[0] * panel, panel), panel)
    weight = both_ref[:, rows:]
    mixed = jnp.dot(weight, all_ref[...], preferred_element_type=F32)
    mix_ref[...] = mixed
    sig = jax.nn.sigmoid(mixed)
    delta = both_ref[:, :rows].astype(F32) * sig * (1.0 + mixed * (1.0 - sig))
    del_ref[...] = delta.astype(BF)
    mine = mix_ref[own, :]
    hid_ref[...] = (mine * jax.nn.sigmoid(mine)).astype(BF)
    mix_ref[...] = lax.dot_general(weight, del_ref[...], (((0,), (0,)), ((), ())), preferred_element_type=F32)
    sent = mix_ref[own, :].astype(BF)
    wgrad = lax.dot_general(
        del_ref[own, :], all_ref[...], (((1,), (1,)), ((), ())), preferred_element_type=F32
    ).astype(BF)
    for z in range(msg_ref.shape[0]):
        for b in range(nblk):
            msg_ref[z, b] = sent[:, b * BLK : (b + 1) * BLK]
        for h in range(msg_ref.shape[1] - nblk):
            msg_ref[z, nblk + h] = wgrad[:, h * BLK : (h + 1) * BLK]


def spread(got_ref, msg_ref):
    pairs, blocks, panel, _ = got_ref.shape
    near, stride = msg_ref.shape[:2]
    nblk = (stride - blocks) // (pairs - 1)
    for h in range(blocks - nblk):
        total = jnp.zeros((panel, BLK), F32)
        for z in range(pairs):
            total += got_ref[z, nblk + h].astype(F32)
        for k in range(near):
            msg_ref[k, pairs * nblk + h] = total.astype(BF)
    for z in range(pairs):
        one = got_ref[z, :nblk]
        for k in range(near):
            msg_ref[k, z * nblk : (z + 1) * nblk] = one


def per_device(feats, weight, tile_values, tile_dest, tile_block, tile_source, cotangent):
    panel, rows = feats.shape
    tiles = tile_values.shape[0]
    nblk = rows // BLK
    ntot = NY * NZ * nblk
    near = NY * NP
    full = NX * NC * panel
    halves = full // BLK
    stride = NZ8 * nblk + halves
    shape = jax.ShapeDtypeStruct
    tile_bytes = tiles * BLK * BLK * 2
    tile_flops = 2 * tiles * panel * BLK * BLK
    rep = lax.axis_index(("x", "core")).astype(jnp.int32).reshape(1)
    places = (rep, *map(in_hbm, (tile_dest[:, 0], tile_block, tile_source)))

    parts = call(
        scatter_products,
        "scatter_products",
        pltpu.HBM((ntot, panel, BLK), BF),
        [SMEM, SMEM, SMEM, SMEM, VMEM, HBM],
        [
            pltpu.VMEM((ntot, panel, BLK), F32),
            pltpu.VMEM((ntot, panel, BLK), BF),
            pltpu.VMEM((tiles, BLK, BLK), BF),
            pltpu.SemaphoreType.DMA((len(CHUNKS),)),
            pltpu.SemaphoreType.DMA((WRITES,)),
        ],
        flops=tile_flops,
        nbytes=tile_bytes,
        outs=HBM,
    )(*places, in_hbm(feats), in_hbm(tile_values))

    got = exchange(parts.reshape(near, NZ8 * nblk, panel, BLK), ("y", "zp"), NEAR_ORDER, NEAR_TURN)
    both = lax.all_gather(
        jnp.concatenate([cotangent, weight.T], axis=1), ("x", "core"), axis=0, tiled=True
    )
    got, both = lax.optimization_barrier((got, both))
    half = call(sum_first, "sum_near", shape((NZ8 * nblk, panel, BLK), BF), [VMEM], nbytes=ntot * panel * BLK * 2)(got)
    got = exchange(half.reshape(NZ8, nblk, panel, BLK), ("z8",), FAR_ORDER, FAR_TURN)
    mine = call(finish_sum, "sum_far", shape((NX, nblk, panel, BLK), BF), [VMEM], nbytes=1 << 19)(got)
    gathered = lax.all_gather(exchange(mine, ("x",), X_ORDER), "core", axis=0)

    hidden, sent = call(
        middle,
        "middle",
        (
            shape((panel, rows), BF),
            shape((NZ8, nblk + halves, panel, BLK), BF),
        ),
        [SMEM, VMEM, VMEM],
        [pltpu.VMEM((full, rows), BF), pltpu.VMEM((full, rows), BF), pltpu.VMEM((full, rows), F32)],
        flops=6 * full * full * rows,
        nbytes=1 << 20,
    )(rep, gathered, both)

    col = exchange(sent, ("z8",), FAR_ORDER, FAR_TURN)
    copies = call(
        spread,
        "spread",
        shape((near, stride, panel, BLK), BF),
        [VMEM],
        nbytes=ntot * panel * BLK * 2,
    )(col)
    every = exchange(copies, ("y", "zp"), NEAR_ORDER, NEAR_TURN)

    input_grad, weight_grad = call(
        gather_products,
        "gather_products",
        (shape((panel, rows), BF), shape((panel, full), F32)),
        [SMEM, SMEM, SMEM, SMEM, VMEM, VMEM],
        [pltpu.VMEM((nblk, panel, BLK), F32)],
        flops=tile_flops,
        nbytes=tile_bytes,
    )(*places, every.reshape(near * stride, panel, BLK), tile_values)
    return hidden, weight_grad.T, input_grad


def solution(mesh):
    split = Mesh(mesh.devices.reshape(NY, NZ8, NP, NX, NC), ("y", "z8", "zp", "x", "core"))
    dom, rep = ("y", "z8", "zp"), ("x", "core")
    placed = (P(rep, dom), P(None, rep), P(dom, None, None), P(dom, None), P(dom), P(dom), P(rep, dom))
    return jax.shard_map(
        per_device,
        mesh=split,
        in_specs=placed,
        out_specs=(P(rep, dom), P(None, rep), P(rep, dom)),
        check_vma=False,
    )
```

```python
import math

import jax
import jax.numpy as jnp
import numpy as np
from jax import lax
from jax.experimental import pallas as pl
from jax.experimental.pallas import tpu as pltpu
from jax.sharding import Mesh, PartitionSpec as P

BF = jnp.bfloat16
F32 = jnp.float32
NY, NZ, NX, NC = 4, 16, 4, 2
BLK = 128
CHUNKS = (16, 48, 64)
NZ8, NP = NZ // 2, 2

SMEM = pl.BlockSpec(memory_space=pltpu.SMEM)
VMEM = pl.BlockSpec(memory_space=pltpu.VMEM)
HBM = pl.BlockSpec(memory_space=pltpu.HBM)


def in_hbm(x):
    return pltpu.with_memory_space_constraint(x, pltpu.HBM)


AXES = ("y", "z8", "zp", "x", "core")
SIZES = (NY, NZ8, NP, NX, NC)
NEAR_ORDER = [(0, 0), (1, 0), (2, 0), (3, 0), (0, 1), (1, 1), (2, 1), (3, 1)]
FAR_ORDER = [(0,), (2,), (4,), (6,), (1,), (3,), (5,), (7,)]
NEAR_TURN, FAR_TURN = 4, 7
X_ORDER = [(0,), (2,), (1,), (3,)]


def exchange(x, axes, order, turn=0):
    others = [a for a in AXES if a not in axes]
    ranks = np.arange(math.prod(SIZES)).reshape(SIZES)
    ranks = ranks.transpose([AXES.index(a) for a in (*others, *axes)])
    ranks = ranks.reshape(-1, *(SIZES[AXES.index(a)] for a in axes))
    groups = [[int(r[order[i ^ (turn * (r.flat[0] % NC))]]) for i in range(len(order))] for r in ranks]
    flat = x.reshape(x.shape[0], -1, BLK)
    return lax.all_to_all(flat, AXES, 0, 0, tiled=True, axis_index_groups=groups).reshape(x.shape)


def slot(dest, block, core, nblk, stride):
    y, z = lax.shift_right_logical(dest, 4), dest & 15
    near = ((z & 1) * 4 + y) ^ (core * NEAR_TURN)
    far = ((z & 2) * 2 + lax.shift_right_logical(z, 2)) ^ (core * FAR_TURN)
    return near * stride + far * nblk + block


def call(kernel, name, out_shape, in_specs, scratch=(), mib=24, flops=0, nbytes=0, outs=None):
    outs = outs or jax.tree.map(lambda _: VMEM, out_shape)
    return pl.pallas_call(
        kernel,
        name=name,
        out_shape=out_shape,
        in_specs=in_specs,
        out_specs=outs,
        scratch_shapes=list(scratch),
        compiler_params=pltpu.CompilerParams(vmem_limit_bytes=mib << 20),
        cost_estimate=pl.CostEstimate(flops=flops, bytes_accessed=nbytes, transcendentals=0),
    )


def scatter_products(
    rep_ref, dest_ref, block_ref, src_ref, feats_ref, tiles_ref, out_ref, acc_ref, buf_ref, sems
):
    copies = []
    for c, n in enumerate(CHUNKS):
        part = pl.ds(sum(CHUNKS[:c]), n)
        copies.append(pltpu.make_async_copy(tiles_ref.at[part], buf_ref.at[part], sems.at[c]))
        copies[c].start()
    acc_ref[...] = jnp.zeros_like(acc_ref)
    nblk = feats_ref.shape[1] // BLK
    for c, n in enumerate(CHUNKS):
        copies[c].wait()
        for t in range(sum(CHUNKS[:c]), sum(CHUNKS[:c]) + n):
            col = pl.multiple_of(src_ref[t] * BLK, BLK)
            prod = lax.dot_general(
                feats_ref[:, pl.ds(col, BLK)],
                buf_ref[t],
                (((1,), (1,)), ((), ())),
                preferred_element_type=F32,
            )
            acc_ref[slot(dest_ref[t], block_ref[t], rep_ref[0] & 1, nblk, NZ8 * nblk)] += prod
    out_ref[...] = acc_ref[...].astype(BF)


def gather_products(rep_ref, dest_ref, block_ref, src_ref, every_ref, tiles_ref, out_ref, wg_ref, acc_ref):
    acc_ref[...] = jnp.zeros_like(acc_ref)
    nblk, panel, _ = acc_ref.shape
    stride = every_ref.shape[0] // (NY * NP)
    for h in range(stride - NZ8 * nblk):
        total = jnp.zeros((panel, BLK), F32)
        for k in range(NY * NP):
            total += every_ref[k * stride + NZ8 * nblk + h].astype(F32)
        wg_ref[:, h * BLK : (h + 1) * BLK] = total * float(nblk * BLK * NY * NZ) ** (-0.5)
    for t in range(tiles_ref.shape[0]):
        prod = jnp.dot(
            every_ref[slot(dest_ref[t], block_ref[t], rep_ref[0] & 1, nblk, stride)], tiles_ref[t], preferred_element_type=F32
        )
        acc_ref[src_ref[t]] += prod
    for b in range(nblk):
        out_ref[:, b * BLK : (b + 1) * BLK] = acc_ref[b].astype(BF)


def sum_first(got_ref, out_ref):
    total = got_ref[0].astype(F32)
    for k in range(1, got_ref.shape[0]):
        total += got_ref[k].astype(F32)
    out_ref[...] = total.astype(BF)


def finish_sum(got_ref, out_ref):
    for b in range(got_ref.shape[1]):
        total = got_ref[0, b].astype(F32)
        for k in range(1, got_ref.shape[0]):
            total += got_ref[k, b].astype(F32)
        total = total.astype(BF)
        for r in range(out_ref.shape[0]):
            out_ref[r, b] = total


def middle(rep_ref, got_ref, both_ref, hid_ref, msg_ref, all_ref, del_ref, mix_ref):
    cores, chips, nblk, panel, _ = got_ref.shape
    rows = nblk * BLK
    for r in range(cores * chips):
        for b in range(nblk):
            all_ref[r * panel : (r + 1) * panel, b * BLK : (b + 1) * BLK] = got_ref[r % cores, [m[0] for m in X_ORDER].index(r // cores), b]
    own = pl.ds(pl.multiple_of(rep_ref[0] * panel, panel), panel)
    weight = both_ref[:, rows:]
    mixed = jnp.dot(weight, all_ref[...], preferred_element_type=F32)
    mix_ref[...] = mixed
    sig = jax.nn.sigmoid(mixed)
    delta = both_ref[:, :rows].astype(F32) * sig * (1.0 + mixed * (1.0 - sig))
    del_ref[...] = delta.astype(BF)
    mine = mix_ref[own, :]
    hid_ref[...] = (mine * jax.nn.sigmoid(mine)).astype(BF)
    mix_ref[...] = lax.dot_general(weight, del_ref[...], (((0,), (0,)), ((), ())), preferred_element_type=F32)
    sent = mix_ref[own, :].astype(BF)
    wgrad = lax.dot_general(
        del_ref[own, :], all_ref[...], (((1,), (1,)), ((), ())), preferred_element_type=F32
    ).astype(BF)
    for z in range(msg_ref.shape[0]):
        for b in range(nblk):
            msg_ref[z, b] = sent[:, b * BLK : (b + 1) * BLK]
        for h in range(msg_ref.shape[1] - nblk):
            msg_ref[z, nblk + h] = wgrad[:, h * BLK : (h + 1) * BLK]


def spread(got_ref, msg_ref):
    pairs, blocks, panel, _ = got_ref.shape
    near, stride = msg_ref.shape[:2]
    nblk = (stride - blocks) // (pairs - 1)
    for h in range(blocks - nblk):
        total = jnp.zeros((panel, BLK), F32)
        for z in range(pairs):
            total += got_ref[z, nblk + h].astype(F32)
        for k in range(near):
            msg_ref[k, pairs * nblk + h] = total.astype(BF)
    for z in range(pairs):
        one = got_ref[z, :nblk]
        for k in range(near):
            msg_ref[k, z * nblk : (z + 1) * nblk] = one


def per_device(feats, weight, tile_values, tile_dest, tile_block, tile_source, cotangent):
    panel, rows = feats.shape
    tiles = tile_values.shape[0]
    nblk = rows // BLK
    ntot = NY * NZ * nblk
    near = NY * NP
    full = NX * NC * panel
    halves = full // BLK
    stride = NZ8 * nblk + halves
    shape = jax.ShapeDtypeStruct
    tile_bytes = tiles * BLK * BLK * 2
    tile_flops = 2 * tiles * panel * BLK * BLK
    rep = lax.axis_index(("x", "core")).astype(jnp.int32).reshape(1)
    places = (rep, *map(in_hbm, (tile_dest[:, 0], tile_block, tile_source)))

    parts = call(
        scatter_products,
        "scatter_products",
        shape((ntot, panel, BLK), BF),
        [SMEM, SMEM, SMEM, SMEM, VMEM, HBM],
        [
            pltpu.VMEM((ntot, panel, BLK), F32),
            pltpu.VMEM((tiles, BLK, BLK), BF),
            pltpu.SemaphoreType.DMA((len(CHUNKS),)),
        ],
        flops=tile_flops,
        nbytes=tile_bytes,
    )(*places, in_hbm(feats), in_hbm(tile_values))

    got = exchange(parts.reshape(near, NZ8 * nblk, panel, BLK), ("y", "zp"), NEAR_ORDER, NEAR_TURN)
    half = call(sum_first, "sum_near", shape((NZ8 * nblk, panel, BLK), BF), [VMEM], nbytes=ntot * panel * BLK * 2)(got)
    cot, weight_t, half = lax.optimization_barrier((cotangent, weight.T, half))
    got = exchange(half.reshape(NZ8, nblk, panel, BLK), ("z8",), FAR_ORDER, FAR_TURN)
    both = lax.all_gather(jnp.concatenate([cot, weight_t], axis=1), ("x", "core"), axis=0, tiled=True)
    got, both = lax.optimization_barrier((got, both))
    mine = call(finish_sum, "sum_far", shape((NX, nblk, panel, BLK), BF), [VMEM], nbytes=1 << 19)(got)
    gathered = lax.all_gather(exchange(mine, ("x",), X_ORDER), "core", axis=0)

    hidden, sent = call(
        middle,
        "middle",
        (
            shape((panel, rows), BF),
            shape((NZ8, nblk + halves, panel, BLK), BF),
        ),
        [SMEM, VMEM, VMEM],
        [pltpu.VMEM((full, rows), BF), pltpu.VMEM((full, rows), BF), pltpu.VMEM((full, rows), F32)],
        flops=6 * full * full * rows,
        nbytes=1 << 20,
    )(rep, gathered, both)

    col = exchange(sent, ("z8",), FAR_ORDER, FAR_TURN)
    copies = call(
        spread,
        "spread",
        shape((near, stride, panel, BLK), BF),
        [VMEM],
        nbytes=ntot * panel * BLK * 2,
    )(col)
    every = exchange(copies, ("y", "zp"), NEAR_ORDER, NEAR_TURN)

    input_grad, weight_grad = call(
        gather_products,
        "gather_products",
        (shape((panel, rows), BF), shape((panel, full), F32)),
        [SMEM, SMEM, SMEM, SMEM, VMEM, VMEM],
        [pltpu.VMEM((nblk, panel, BLK), F32)],
        flops=tile_flops,
        nbytes=tile_bytes,
    )(*places, every.reshape(near * stride, panel, BLK), tile_values)
    return hidden, weight_grad.T, input_grad


def solution(mesh):
    split = Mesh(mesh.devices.reshape(NY, NZ8, NP, NX, NC), ("y", "z8", "zp", "x", "core"))
    dom, rep = ("y", "z8", "zp"), ("x", "core")
    placed = (P(rep, dom), P(None, rep), P(dom, None, None), P(dom, None), P(dom), P(dom), P(rep, dom))
    return jax.shard_map(
        per_device,
        mesh=split,
        in_specs=placed,
        out_specs=(P(rep, dom), P(None, rep), P(rep, dom)),
        check_vma=False,
    )
```
